256 devices in a mesh: seq: 32 (over z, x_lo, core), chan: 8 (over x_hi, y).
Axes of the slice: x: 4 (x_hi: 2, x_lo: 2; x = x_hi * 2 + x_lo), y: 4, z: 8, core: 2. Of those that a mesh axis runs over, the one named last changes fastest.
Arguments:
- tokens: bfloat16 [8192, 4096], P('seq'), may hold values from -6 to 6
- w_in: bfloat16 [4096, 3, 4096], P('seq', None, 'chan'), may hold values from -0.09375 to 0.09375
- short_taps: float32 [3, 3, 4096], P(None, None, 'chan'), may hold values from -3.5 to 3.5
- residues: float32 [16, 4096], P(None, 'chan'), may hold values from -6 to 6
- decay_rates: float32 [16, 4096], P(None, 'chan'), may hold values from 3.0517578e-05 to 0.05
- skip_gain: float32 [4096], P('chan'), may hold values from -4 to 4
- w_out: bfloat16 [4096, 4096], P('chan'), may hold values from -0.125 to 0.125
Outputs:
- operator_out: bfloat16 [8192, 4096], P('seq', 'chan')
The draws below stay inside these ranges and needn't reach their ends.
All inputs are finite; a program needn't handle non-finite values.
Results may differ from the reference program's by a relative error of at most 0.015.
Values may be sent and summed in bfloat16 or wider, within the bound.
A program may use at most 128 MiB of HBM per device.

```python
import math
import jax
import jax.numpy as jnp
from jax import lax

D = 4096
MODES = 16
TOKENS = 8192


def raised(values, own_key, source, target, shards_of, factor):
    def block_of(position):
        return (jnp.arange(values.shape[position]) // (values.shape[position] // shards_of)).reshape((-1,) + (1,) * (values.ndim - 1 - position))

    one_side = jax.random.permutation(own_key, shards_of)[block_of(target)]
    other_side = (block_of(target) + shards_of // 2) % shards_of
    return jnp.where((block_of(source) == one_side) | (block_of(source) == other_side), factor * values, values)


def steps_of(key, shape, split, least, high):
    def one(axis_at, shards_of):
        heights = jax.random.uniform(jax.random.fold_in(jax.random.fold_in(key, 6), axis_at), (shards_of,), jnp.float32, least / len(split), high / len(split))
        return jnp.repeat(jnp.exp(heights), shape[axis_at] // shards_of).reshape((-1,) + (1,) * (len(shape) - axis_at - 1))

    factor_of = one(*split[0])
    for cut in split[1:]:
        factor_of = factor_of * one(*cut)
    return factor_of


def noise(key, extent, width, most, pieces=(), held_as=jnp.bfloat16):
    level = steps_of(key, extent, pieces, -0.22, 0.18) if pieces else 1.0
    array = jax.random.normal(key, extent, jnp.float32) * width * level
    return jnp.minimum(jnp.maximum(array, -most), most).astype(held_as)


def bell_draw_with(stream_key, extent, spread, bound, cuts, heavy, kind=jnp.bfloat16):
    values = spread * jax.random.normal(stream_key, extent, jnp.float32)
    if cuts:
        values = values * steps_of(stream_key, extent, cuts, -0.22, 0.18)
    return jnp.clip(raised(values, jax.random.fold_in(stream_key, 3), *heavy), -bound, bound).astype(kind)


def setup_inputs(seed: int = 0) -> dict:
    splits = jax.random.split(jax.random.key(seed), 8)
    return {
        "tokens": noise(splits[0], (TOKENS, D), 1.0, 6.0, ((0, 32),)),
        "w_in": noise(splits[1], (D, 3, D), D ** -0.5, 0.09375, ((0, 32), (2, 8))),
        "short_taps": noise(splits[2], (3, 3, D), 3 ** -0.5, 3.5, ((2, 8),), jnp.float32),
        "residues": noise(splits[3], (MODES, D), 1.0, 6.0, ((1, 8),), jnp.float32),
        "decay_rates": jnp.clip(jnp.exp(math.log(0.05) - 7.4014754 * jax.random.uniform(splits[4], (MODES, D), jnp.float32) ** steps_of(splits[4], (MODES, D), ((1, 8),), -0.2, 0.2)), 3.0517578125e-05, 0.05),
        "skip_gain": noise(splits[5], (D,), 1.0, 4.0, ((0, 8),), jnp.float32),
        "w_out": bell_draw_with(splits[6], (D, D), D ** -0.5, 0.125, ((0, 8),), (0, 1, 8, 2.0)),
    }


def reference(tokens, w_in, short_taps, residues, decay_rates, skip_gain, w_out):
    length = tokens.shape[0]
    model_width = tokens.shape[1]
    projected = jnp.dot(tokens, w_in.reshape(model_width, 3 * model_width), preferred_element_type=jnp.float32)
    rounded = lax.optimization_barrier(projected.astype(jnp.bfloat16))
    streams = rounded.astype(jnp.float32).reshape(length, 3, model_width)
    padded = jnp.concatenate([jnp.zeros((2, 3, model_width), jnp.float32), streams], 0)
    shorted = short_taps[0] * padded[2:] + short_taps[1] * padded[1:length + 1] + short_taps[2] * padded[:length]
    product = shorted[:, 1] * shorted[:, 2]
    amplitude = residues * jnp.sqrt(2.0 * decay_rates / residues.shape[0])
    positions = jnp.arange(length, dtype=jnp.float32)

    def add_mode(mode_index, kernel):
        return kernel + amplitude[mode_index] * jnp.exp(-(decay_rates[mode_index] * positions[:, None]))
    kernel = lax.fori_loop(0, residues.shape[0], add_mode, jnp.zeros((length, model_width), jnp.float32))
    spectrum = jnp.fft.rfft(product, n=2 * length, axis=0) * jnp.fft.rfft(kernel, n=2 * length, axis=0)
    long_conv = jnp.fft.irfft(spectrum, n=2 * length, axis=0)[:length].astype(jnp.float32)
    gated_out = (shorted[:, 0] * (long_conv + skip_gain * product)).astype(jnp.bfloat16)
    return jnp.dot(gated_out, w_out, preferred_element_type=jnp.float32).astype(jnp.bfloat16)
```

```python
import functools

import jax
import jax.numpy as jnp
from jax import lax
from jax.experimental import pallas as pl
from jax.experimental.pallas import tpu as pltpu
from jax.sharding import PartitionSpec as P

MESH = pl.DeviceIdType.MESH
F32, BF16 = jnp.float32, jnp.bfloat16

PLANES = 8
YS = 4
SLABS = 32
CHANS = 8
CHUNKS = 4
LANES = 128
WIDE = 3 * LANES
DEPTH = 4096
BLOCK = DEPTH // SLABS
HALF = BLOCK // 2
ROWS = 256
HALO = 16
SEGS = 8
SEG = ROWS // SEGS
MODES = 16


def copied(ref, sem):
    pltpu.make_async_copy(ref, ref, sem).wait()


def kernel(
    tokens, w_in, taps, residues, decays, skip, w_out, out,
    wbuf, tok, wt, pj, sh0, prod, ylocal, hseg, est, pst, gated, acc,
    local_sem, w_send, w_major, w_minor, w_cross, w_inject, w_core,
    halo_sem, est_send, est_recv, pst_send, pst_recv, gate_send, gate_recv,
    wt_send, wt_recv, wt_core, wt_core_send,
):
    slab, chan = lax.axis_index("seq"), lax.axis_index("chan")
    z, spot = slab // 4, lax.rem(slab, 4)
    x, core = spot // 2, lax.rem(spot, 2)
    xhi, y = chan // YS, lax.rem(chan, YS)
    sign = 1 - 2 * core

    def at(z_, x_, core_, xhi_, y_):
        return (z_ * 4 + x_ * 2 + core_, xhi_ * YS + y_)

    def turned(distance):
        return lax.rem(z + distance * sign + 2 * PLANES, PLANES)

    ahead, behind = at(turned(1), x, core, xhi, y), at(turned(-1), x, core, xhi, y)
    beside, twin = at(z, 1 - x, core, xhi, y), at(z, x, 1 - core, xhi, y)
    across = at(z, x, core, 1 - xhi, y)
    planes = [at(lax.rem(z + d, PLANES), x, core, xhi, y) for d in range(1, PLANES)]
    mates = [at(z, x, 1 - core, xhi, y), at(z, 1 - x, core, xhi, y), at(z, 1 - x, 1 - core, xhi, y)]
    mate_spots = [x * 2 + 1 - core, (1 - x) * 2 + core, (1 - x) * 2 + 1 - core]
    next_slab = (lax.rem(slab + 1, SLABS), chan)
    prev_slab = (lax.rem(slab + SLABS - 1, SLABS), chan)
    y_mates = [lax.rem(y + d, YS) for d in (1, 3, 2)]
    diagonals = [at(z, 1 - x, core, 1 - xhi, y_) for y_ in range(YS)]

    def start(src, dst, send, recv, device):
        pltpu.make_async_remote_copy(
            src_ref=src, dst_ref=dst, send_sem=send, recv_sem=recv, device_id=device, device_id_type=MESH
        ).start()


    def rows(c, z_, x_, core_, first, count):
        begin = pl.multiple_of((z_ * 4 + x_ * 2 + core_) * BLOCK + first, HALF)
        return wbuf.at[c, pl.ds(begin, count)]

    def w_copy(c, ref, device, recv):
        start(ref, ref, w_send.at[c], recv, device)

    def main_rows(c, z_):
        return rows(c, z_, x, core, 0, BLOCK)

    def carried_rows(c, z_):
        return rows(c, z_, 1 - x, core, 0, HALF)

    def to_core(c, ref):
        w_copy(c, ref, twin, w_core.at[c])

    def own_first(c):
        w_copy(c, rows(c, z, x, core, 0, HALF), beside, w_inject.at[c])
        w_copy(c, main_rows(c, z), ahead, w_major.at[c, 0, 0])
        w_copy(c, main_rows(c, z), behind, w_minor.at[c, 0, 0])
        w_copy(c, rows(c, z, x, core, HALF, HALF), beside, w_cross.at[c, 0])
        to_core(c, main_rows(c, z))

    def own_second(c):
        block = carried_rows(c, z)
        copied(block, w_inject.at[c])
        w_copy(c, block, ahead, w_major.at[c, 0, 1])
        w_copy(c, block, behind, w_minor.at[c, 0, 1])
        to_core(c, block)

    def ring(c, j):
        for part, of in ((0, main_rows), (1, carried_rows)):
            for sems, device, last, source, place in (
                (w_major, ahead, 4, turned(-j), j),
                (w_minor, behind, 3, turned(j), 4 + j),
            ):
                if j > last:
                    continue
                block = of(c, source)
                copied(block, sems.at[c, j - 1, part])
                if j < last:
                    w_copy(c, block, device, sems.at[c, j, part])
                if part == 0:
                    w_copy(c, rows(c, source, x, core, HALF, HALF), beside, w_cross.at[c, place])
                to_core(c, block)

    def cross(c, j):
        places = [(z, 0)] if j == 0 else [(turned(-j), j)] + ([(turned(j), 4 + j)] if j < 4 else [])
        for source, place in places:
            block = rows(c, source, 1 - x, core, HALF, HALF)
            copied(block, w_cross.at[c, place])
            to_core(c, block)


    w_out_chunks = w_out.reshape(CHUNKS, LANES, DEPTH)
    mine = pl.ds(core * 2, 2)

    def wt_slot(part, source):
        return wt.at[part, pl.ds(pl.multiple_of(source * LANES, LANES), LANES)]

    def wt_columns(part, target):
        return w_out_chunks.at[part, :, pl.ds(pl.multiple_of(target * 512, 512), 512)]

    wt_peers = [(xhi * YS + y_, at(z, x, core, xhi, y_)) for y_ in y_mates]
    wt_peers += [((1 - xhi) * YS + y_, diagonals[y_]) for y_ in range(YS)]

    def wt_start():
        for target, device in wt_peers:
            start(wt_columns(mine, target), wt_slot(mine, chan), wt_send, wt_recv.at[chan], device)

    def wt_relay():
        for source, _ in wt_peers:
            copied(wt_slot(mine, source), wt_recv.at[source])
            start(wt_slot(mine, source), wt_slot(mine, source), wt_core_send, wt_core, twin)


    def lanes(ref, row, c):
        return ref[pl.ds(row, 1), c * LANES:(c + 1) * LANES]

    def wait_w(c):
        copied(wbuf.at[c, pl.ds(0, DEPTH // 2)], w_core.at[c])

    def project(c):
        result = jnp.dot(tok[...], wbuf[c], preferred_element_type=F32)
        pj[...] = result.astype(BF16).astype(F32)

        @pl.when(slab == 0)
        def _():
            pj[pl.ds(0, HALO)] = jnp.zeros((HALO, WIDE), F32)

    def shorten(c):
        def stream(j):
            total = None
            for a in range(3):
                term = lanes(taps, a * 3 + j, c) * pj[pl.ds(HALO - a, ROWS), j * LANES:(j + 1) * LANES]
                total = term if total is None else total + term
            return total

        sh0[c] = stream(0)
        prod[c] = stream(1) * stream(2)

    def mode_lanes(c, m):
        rate = jnp.broadcast_to(lanes(decays, m, c), (SEGS, LANES))
        size = jnp.broadcast_to(lanes(residues, m, c), (SEGS, LANES))
        return rate, size

    def recur(c):
        factors, gains = [], []
        for m in range(MODES):
            rate, size = mode_lanes(c, m)
            factors.append(jnp.exp(-rate))
            gains.append(size * jnp.sqrt(rate * (2.0 / MODES)))

        def step(i, states):
            value = prod[c, pl.ds(i, SEGS, stride=SEG), :]
            states = tuple(f * s + g * value for f, g, s in zip(factors, gains, states))
            parts = list(states)
            while len(parts) > 1:
                parts = [a + b for a, b in zip(parts[::2], parts[1::2])]
            ylocal[c, pl.ds(i, SEGS, stride=SEG), :] = parts[0]
            return states

        states = lax.fori_loop(0, SEG, step, (jnp.zeros((SEGS, LANES), F32),) * MODES, unroll=4)
        segment = lax.broadcasted_iota(jnp.int32, (SEGS, LANES), 0)
        for m in range(MODES):
            rate, _ = mode_lanes(c, m)
            total = states[m]
            for shift in (1, 2, 4):
                earlier = jnp.where(segment >= shift, pltpu.roll(total, shift, 0), 0.0)
                total = total + jnp.exp(rate * (-float(SEG * shift))) * earlier
            hseg[c, m] = jnp.where(segment >= 1, pltpu.roll(total, 1, 0), 0.0)
            est[c, spot, pl.ds(m, 1)] = total[SEGS - 1:]

    def send_states(c):
        block = est.at[c, spot]
        for device in mates:
            start(block, block, est_send.at[c], est_recv.at[c, spot], device)

    def slab_factor(c, slabs):
        return jnp.exp(decays[:, c * LANES:(c + 1) * LANES] * (-float(ROWS * slabs)))

    def plane_states(c):
        for place in mate_spots:
            copied(est.at[c, place], est_recv.at[c, place])
        factor = slab_factor(c, 1)
        total = est[c, 0]
        for q in range(1, 4):
            total = factor * total + est[c, q]
        pst[c, z] = total
        block = pst.at[c, z]

        def pass_on(later, _):
            start(block, block, pst_send.at[c, later], pst_recv.at[c, z], at(later, x, core, xhi, y))
            return 0

        lax.fori_loop(z + 1, PLANES, pass_on, 0)

    def finish(c):
        factor, plane_factor = slab_factor(c, 1), slab_factor(c, 4)

        def gather(earlier, total):
            copied(pst.at[c, earlier], pst_recv.at[c, earlier])
            return plane_factor * total + pst[c, earlier]

        total = lax.fori_loop(0, z, gather, jnp.zeros((MODES, LANES), F32))
        for q in range(3):
            total = jnp.where(q < spot, factor * total + est[c, q], total)
        segment = lax.broadcasted_iota(jnp.int32, (SEGS, LANES), 0).astype(F32)
        factors, states = [], []
        for m in range(MODES):
            rate, _ = mode_lanes(c, m)
            factors.append(jnp.exp(-rate))
            entering = jnp.exp(rate * (segment * -float(SEG))) * jnp.broadcast_to(total[m:m + 1], (SEGS, LANES))
            states.append(hseg[c, m] + entering)

        def step(i, states):
            states = tuple(f * s for f, s in zip(factors, states))
            parts = list(states)
            while len(parts) > 1:
                parts = [a + b for a, b in zip(parts[::2], parts[1::2])]
            place = pl.ds(i, SEGS, stride=SEG)
            ylocal[c, place, :] = ylocal[c, place, :] + parts[0]
            return states

        lax.fori_loop(0, SEG, step, tuple(states), unroll=4)
        value = sh0[c] * (ylocal[c] + lanes(skip, 0, c) * prod[c])
        gated[c, :, pl.ds(pl.multiple_of(chan * LANES, LANES), LANES)] = value.astype(BF16)

    def gate_slot(c, source):
        return gated.at[c, :, pl.ds(pl.multiple_of(source * LANES, LANES), LANES)]

    def send_gated(c, source, also_across):
        block = gate_slot(c, source)
        if also_across:
            start(block, block, gate_send.at[c], gate_recv.at[c, source], across)
        for y_ in y_mates:
            start(block, block, gate_send.at[c], gate_recv.at[c, source], at(z, x, core, xhi, y_))

    def relay_gated(c):
        source = (1 - xhi) * YS + y
        copied(gate_slot(c, source), gate_recv.at[c, source])
        send_gated(c, source, False)

    def add_out(c):
        for y_ in y_mates:
            for xhi_ in (xhi, 1 - xhi):
                source = xhi_ * YS + y_
                copied(gate_slot(c, source), gate_recv.at[c, source])
        part = jnp.dot(gated[c], wt[c], preferred_element_type=F32)
        if c == 0:
            acc[...] = part
        elif c < CHUNKS - 1:
            acc[...] += part
        else:
            out[...] = (acc[...] + part).astype(BF16)


    for c in range(CHUNKS):
        for j in range(3):
            pltpu.make_async_copy(
                w_in.at[j, :, c * LANES:(c + 1) * LANES],
                rows(c, z, x, core, 0, BLOCK).at[:, j * LANES:(j + 1) * LANES],
                local_sem.at[c],
            ).start()
    own_tokens = pltpu.make_async_copy(tokens, tok.at[pl.ds(HALO, ROWS)], local_sem.at[CHUNKS])
    own_tokens.start()
    own_columns = pltpu.make_async_copy(
        wt_columns(slice(None), chan), wt_slot(slice(None), chan), local_sem.at[CHUNKS + 1]
    )
    own_columns.start()

    barrier = pltpu.get_barrier_semaphore()
    greeted = planes + mates + [next_slab, prev_slab, across] + diagonals
    greeted += [at(z, x, core, xhi, y_) for y_ in y_mates]
    for device in greeted:
        pl.semaphore_signal(barrier, inc=1, device_id=device, device_id_type=MESH)
    pl.semaphore_wait(barrier, len(greeted))

    for c in range(CHUNKS):
        copied(main_rows(c, z), local_sem.at[c])

    def operator_parts(c):
        first = 2 * c + 6
        return {
            first: [lambda: (wait_w(c), project(c), shorten(c), recur(c), send_states(c))],
            first + 1: [lambda: plane_states(c)],
            first + 2: [lambda: (finish(c), send_gated(c, chan, True))],
            first + 3: [lambda: relay_gated(c)],
            first + 4: [lambda: add_out(c)],
        }

    work = {}
    for c in range(CHUNKS):
        for when, parts in operator_parts(c).items():
            work.setdefault(when, []).extend(parts)

    for t in range(2 * CHUNKS + 10):
        opened = t // 2 if t % 2 == 0 and t // 2 < CHUNKS else None
        if opened is not None:
            own_first(opened)
        for c in range(CHUNKS):
            if 1 <= t - 2 * c <= 4:
                ring(c, t - 2 * c)
        if opened is not None:
            own_second(opened)
        for c in range(CHUNKS):
            if 1 <= t - 2 * c <= 5:
                cross(c, t - 2 * c - 1)
        if t == 0:
            start(tokens.at[pl.ds(ROWS - HALO, HALO)], tok.at[pl.ds(0, HALO)], halo_sem.at[0], halo_sem.at[1], next_slab)
            wt_start()
        if t == 5:
            own_tokens.wait()
            copied(tok.at[pl.ds(0, HALO)], halo_sem.at[1])
        if t == 9:
            own_columns.wait()
            wt_relay()
            copied(wt.at[mine, pl.ds(0, 7 * LANES)], wt_core)
        for part in work.get(t, []):
            part()

    copied(tok.at[pl.ds(0, HALO)], halo_sem.at[0])
    copied(wt.at[mine, pl.ds(0, 7 * LANES)], wt_send)
    copied(wt.at[mine, pl.ds(0, 7 * LANES)], wt_core_send)
    for c in range(CHUNKS):
        copied(wbuf.at[c, pl.ds(0, 7 * (BLOCK + HALF) + 9 * HALF + DEPTH // 2)], w_send.at[c])
        copied(est.at[c, pl.ds(0, 3)], est_send.at[c])
        copied(gated.at[c, :, pl.ds(0, 7 * LANES)], gate_send.at[c])

        def sent(later, _):
            copied(pst.at[c, z], pst_send.at[c, later])
            return 0

        lax.fori_loop(z + 1, PLANES, sent, 0)


def body(tokens, w_in, short_taps, residues, decay_rates, skip_gain, w_out):
    any_space = pl.BlockSpec(memory_space=pl.ANY)
    vmem = pl.BlockSpec(memory_space=pltpu.VMEM)
    dma = pltpu.SemaphoreType.DMA
    width = CHUNKS * LANES
    return pl.pallas_call(
        kernel,
        out_shape=jax.ShapeDtypeStruct((ROWS, width), BF16),
        in_specs=[any_space, any_space, vmem, vmem, vmem, vmem, any_space],
        out_specs=vmem,
        scratch_shapes=[
            pltpu.VMEM((CHUNKS, DEPTH, WIDE), BF16),
            pltpu.VMEM((HALO + ROWS, DEPTH), BF16),
            pltpu.VMEM((CHUNKS, CHANS * LANES, width), BF16),
            pltpu.VMEM((HALO + ROWS, WIDE), F32),
            pltpu.VMEM((CHUNKS, ROWS, LANES), F32),
            pltpu.VMEM((CHUNKS, ROWS, LANES), F32),
            pltpu.VMEM((CHUNKS, ROWS, LANES), F32),
            pltpu.VMEM((CHUNKS, MODES, SEGS, LANES), F32),
            pltpu.VMEM((CHUNKS, 4, MODES, LANES), F32),
            pltpu.VMEM((CHUNKS, PLANES, MODES, LANES), F32),
            pltpu.VMEM((CHUNKS, ROWS, CHANS * LANES), BF16),
            pltpu.VMEM((ROWS, width), F32),
            dma((CHUNKS + 2,)),
            dma((CHUNKS,)),
            dma((CHUNKS, 4, 2)),
            dma((CHUNKS, 3, 2)),
            dma((CHUNKS, 8)),
            dma((CHUNKS,)),
            dma((CHUNKS,)),
            dma((2,)),
            dma((CHUNKS,)),
            dma((CHUNKS, 4)),
            dma((CHUNKS, PLANES)),
            dma((CHUNKS, PLANES)),
            dma((CHUNKS,)),
            dma((CHUNKS, CHANS)),
            dma,
            dma((CHANS,)),
            dma,
            dma,
        ],
        compiler_params=pltpu.CompilerParams(
            collective_id=0, has_side_effects=True, vmem_limit_bytes=56 << 20
        ),
        cost_estimate=pl.CostEstimate(flops=5 * 10**9, bytes_accessed=10**7, transcendentals=0),
        name="hyena",
    )(
        tokens,
        w_in.transpose(1, 0, 2),
        short_taps.reshape(9, width),
        residues,
        decay_rates,
        skip_gain.reshape(1, width),
        w_out,
    )


def solution(mesh):
    return jax.shard_map(
        body,
        mesh=mesh,
        in_specs=(
            P("seq", None),
            P("seq", None, "chan"),
            P(None, None, "chan"),
            P(None, "chan"),
            P(None, "chan"),
            P("chan"),
            P("chan", None),
        ),
        out_specs=P("seq", "chan"),
        check_vma=False,
    )
```

```python
import functools

import jax
import jax.numpy as jnp
from jax import lax
from jax.experimental import pallas as pl
from jax.experimental.pallas import tpu as pltpu
from jax.sharding import PartitionSpec as P

MESH = pl.DeviceIdType.MESH
F32, BF16 = jnp.float32, jnp.bfloat16

PLANES = 8
YS = 4
SLABS = 32
CHANS = 8
CHUNKS = 4
LANES = 128
WIDTH = CHUNKS * LANES
DEPTH = 4096
BLOCK = DEPTH // SLABS
HALF = BLOCK // 2
ROWS = 256
HALO = 16
SEGS = 8
SEG = ROWS // SEGS
MODES = 16
UNITS = (
    ((1, 2), 0, 1),
    ((1, 2), 1, 1),
    ((0,), 0, 1),
    ((1, 2), 2, 1),
    ((1, 2), 3, 1),
    ((0,), 1, 1),
    ((0,), 2, 1),
    ((0,), 3, 1),
)
OPENED = (0, 1, 2, 3, 4, 5, 6, 7)
STAGGERED = True
PLANE_LAG, ENTER_LAG, RELAY_LAG, OUT_LAG = 1, 2, 1, 2


def copied(ref, sem):
    pltpu.make_async_copy(ref, ref, sem).wait()


def kernel(
    tokens, w_in, taps_hbm, residues_hbm, decays_hbm, skip_hbm, w_out, out,
    taps, residues, decays, skip, wbufs, tok, wt, pj, sh0, prod, conv, hseg, est, pst, gated, acc,
    local_sem, w_send, w_major, w_minor, w_cross, w_inject, w_core, w_own,
    halo_sem, est_send, est_recv, pst_send, pst_recv, gate_send, gate_recv,
    wt_send, wt_recv, wt_core, wt_core_send,
):
    slab, chan = lax.axis_index("seq"), lax.axis_index("chan")
    z, spot = slab // 4, lax.rem(slab, 4)
    x, core = spot // 2, lax.rem(spot, 2)
    xhi, y = chan // YS, lax.rem(chan, YS)
    sign = 1 - 2 * core

    def at(z_, x_, core_, xhi_, y_):
        return (z_ * 4 + x_ * 2 + core_, xhi_ * YS + y_)

    def turned(distance):
        return lax.rem(z + distance * sign + 2 * PLANES, PLANES)

    ahead, behind = at(turned(1), x, core, xhi, y), at(turned(-1), x, core, xhi, y)
    beside, twin = at(z, 1 - x, core, xhi, y), at(z, x, 1 - core, xhi, y)
    across = at(z, x, core, 1 - xhi, y)
    mates = [at(z, x, 1 - core, xhi, y), at(z, 1 - x, core, xhi, y), at(z, 1 - x, 1 - core, xhi, y)]
    next_slab = (lax.rem(slab + 1, SLABS), chan)
    y_mates = [lax.rem(y + d, YS) for d in (1, 3, 2)]
    diagonals = [at(z, 1 - x, core, 1 - xhi, y_) for y_ in range(YS)]

    def start(src, dst, send, recv, device):
        pltpu.make_async_remote_copy(
            src_ref=src, dst_ref=dst, send_sem=send, recv_sem=recv, device_id=device, device_id_type=MESH
        ).start()


    def rows(c, z_, x_, core_, first, count):
        begin = pl.multiple_of((z_ * 4 + x_ * 2 + core_) * BLOCK + first, HALF)
        return wbufs[c].at[pl.ds(begin, count)]

    def w_copy(c, ref, device, recv):
        start(ref, ref, w_send.at[c], recv, device)

    def main_rows(c, z_):
        return rows(c, z_, x, core, 0, BLOCK)

    def carried_rows(c, z_):
        return rows(c, z_, 1 - x, core, 0, HALF)

    def to_core(c, ref):
        w_copy(c, ref, twin, w_core.at[c])

    def inject(c):
        w_copy(c, rows(c, z, x, core, 0, HALF), beside, w_inject.at[c])

    def own_first(c):
        block = main_rows(c, z)
        start(block, block, w_own.at[c], w_major.at[c, 0, 0], ahead)
        start(block, block, w_own.at[c], w_minor.at[c, 0, 0], behind)
        w_copy(c, rows(c, z, x, core, HALF, HALF), beside, w_cross.at[c])
        to_core(c, main_rows(c, z))

    def own_sent(c):
        copied(wbufs[c].at[pl.ds(0, 2 * BLOCK)], w_own.at[c])

    def own_second(c):
        block = carried_rows(c, z)
        copied(block, w_inject.at[c])
        w_copy(c, block, ahead, w_major.at[c, 0, 1])
        w_copy(c, block, behind, w_minor.at[c, 0, 1])
        to_core(c, block)

    def ring(c, j):
        for part, of in ((0, main_rows), (1, carried_rows)):
            for sems, device, last, source in (
                (w_major, ahead, 4, turned(-j)),
                (w_minor, behind, 3, turned(j)),
            ):
                if j > last:
                    continue
                block = of(c, source)
                copied(block, sems.at[c, j - 1, part])
                if j < last:
                    w_copy(c, block, device, sems.at[c, j, part])
                if part == 0:
                    w_copy(c, rows(c, source, x, core, HALF, HALF), beside, w_cross.at[c])
                to_core(c, block)

    def cross(c):
        copied(wbufs[c].at[pl.ds(0, PLANES * HALF)], w_cross.at[c])
        for source in range(PLANES):
            to_core(c, rows(c, source, 1 - x, core, HALF, HALF))


    w_out_chunks = w_out.reshape(CHUNKS, LANES, DEPTH)
    mine = pl.ds(core * 2, 2)

    def wt_slot(part, source):
        return wt.at[part, pl.ds(pl.multiple_of(source * LANES, LANES), LANES)]

    def wt_columns(part, target):
        return w_out_chunks.at[part, :, pl.ds(pl.multiple_of(target * 512, 512), 512)]

    wt_peers = [(xhi * YS + y_, at(z, x, core, xhi, y_)) for y_ in y_mates]
    wt_peers += [((1 - xhi) * YS + y_, diagonals[y_]) for y_ in range(YS)]

    def wt_start():
        for target, device in wt_peers:
            start(wt_columns(mine, target), wt_slot(mine, chan), wt_send, wt_recv, device)

    def wt_relay():
        copied(wt.at[mine, pl.ds(0, 7 * LANES)], wt_recv)
        for source, _ in wt_peers:
            start(wt_slot(mine, source), wt_slot(mine, source), wt_core_send, wt_core, twin)


    def lanes(ref, row, c):
        return ref[pl.ds(row, 1), c * LANES:(c + 1) * LANES]

    def project(u):
        copied(wbufs[u].at[pl.ds(0, DEPTH // 2)], w_core.at[u])
        width = wbufs[u].shape[1]
        result = jnp.dot(tok[...], wbufs[u][...], preferred_element_type=F32)
        pj[:, :width] = result.astype(BF16).astype(F32)

        @pl.when(slab == 0)
        def _():
            pj[pl.ds(0, HALO), :width] = jnp.zeros((HALO, width), F32)

        streams, first, count = UNITS[u]

        def shorted(j, c):
            column = streams.index(j) * count + c - first
            total = None
            for a in range(3):
                tap = taps[a, pl.ds(j, 1), c * LANES:(c + 1) * LANES]
                term = tap * pj[pl.ds(HALO - a, ROWS), column * LANES:(column + 1) * LANES]
                total = term if total is None else total + term
            return total

        for c in range(first, first + count):
            if 0 in streams:
                sh0[c] = shorted(0, c)
            if 1 in streams:
                prod[c] = shorted(1, c) * shorted(2, c)
                recur(c)
                send_states(c)

    def mode_lanes(c, m):
        rate = jnp.broadcast_to(lanes(decays, m, c), (SEGS, LANES))
        size = jnp.broadcast_to(lanes(residues, m, c), (SEGS, LANES))
        return rate, size

    def added(parts):
        parts = list(parts)
        while len(parts) > 1:
            parts = [a + b for a, b in zip(parts[::2], parts[1::2])]
        return parts[0]

    def recur(c):
        factors, gains = [], []
        for m in range(MODES):
            rate, size = mode_lanes(c, m)
            factors.append(jnp.exp(-rate))
            gains.append(size * jnp.sqrt(rate * (2.0 / MODES)))

        def step(i, states):
            place = pl.ds(i, SEGS, stride=SEG)
            value = prod[c, place, :]
            states = tuple(f * s + g * value for f, g, s in zip(factors, gains, states))
            conv[c, place, :] = added(states)
            return states

        states = lax.fori_loop(0, SEG, step, (jnp.zeros((SEGS, LANES), F32),) * MODES, unroll=4)
        segment = lax.broadcasted_iota(jnp.int32, (SEGS, LANES), 0)
        for m in range(MODES):
            rate, _ = mode_lanes(c, m)
            total = states[m]
            for shift in (1, 2, 4):
                earlier = jnp.where(segment >= shift, pltpu.roll(total, shift, 0), 0.0)
                total = total + jnp.exp(rate * (-float(SEG * shift))) * earlier
            hseg[c, m] = jnp.where(segment >= 1, pltpu.roll(total, 1, 0), 0.0)
            est[c, spot, pl.ds(m, 1)] = total[SEGS - 1:]

    def send_states(c):
        block = est.at[c, spot]
        for device in mates:
            start(block, block, est_send.at[c], est_recv.at[c], device)

    def slab_factor(c, slabs):
        return jnp.exp(decays[:, c * LANES:(c + 1) * LANES] * (-float(ROWS * slabs)))

    def plane_states(c):
        copied(est.at[c, pl.ds(0, 3)], est_recv.at[c])
        factor = slab_factor(c, 1)
        total = est[c, 0]
        for q in range(1, 4):
            total = factor * total + est[c, q]
        pst[c, z] = total
        block = pst.at[c, z]

        for d in (4, 3, 5, 2, 6, 1, 7):
            device = at(lax.rem(z + d, PLANES), x, core, xhi, y)
            start(block, block, pst_send.at[c], pst_recv.at[c], device)

    def enter(c):
        factor, plane_factor = slab_factor(c, 1), slab_factor(c, 4)

        copied(pst.at[c, pl.ds(0, PLANES - 1)], pst_recv.at[c])
        total = jnp.zeros((MODES, LANES), F32)
        for earlier in range(PLANES - 1):
            total = jnp.where(earlier < z, plane_factor * total + pst[c, earlier], total)
        for q in range(3):
            total = jnp.where(q < spot, factor * total + est[c, q], total)
        segment = lax.broadcasted_iota(jnp.int32, (SEGS, LANES), 0).astype(F32)
        factors, states = [], []
        for m in range(MODES):
            rate, _ = mode_lanes(c, m)
            factors.append(jnp.exp(-rate))
            entering = jnp.broadcast_to(total[m:m + 1], (SEGS, LANES))
            states.append(hseg[c, m] + jnp.exp(rate * (segment * -float(SEG))) * entering)

        def step(i, states):
            states = tuple(f * s for f, s in zip(factors, states))
            place = pl.ds(i, SEGS, stride=SEG)
            conv[c, place, :] = conv[c, place, :] + added(states)
            return states

        lax.fori_loop(0, SEG, step, tuple(states), unroll=4)
        conv[c] = conv[c] + lanes(skip, 0, c) * prod[c]

    def gate_slot(c, source):
        return gated.at[c, :, pl.ds(pl.multiple_of(source * LANES, LANES), LANES)]


    def send_across(c, source, part):
        block = gate_slot(c, source)
        start(block, block, gate_send.at[c], gate_recv.at[c, part], across)

    def send_along(c, source, part):
        block = gate_slot(c, source)
        for y_ in y_mates:
            start(block, block, gate_send.at[c], gate_recv.at[c, part], at(z, x, core, xhi, y_))

    def gate(c):
        gated[c, :, pl.ds(pl.multiple_of(chan * LANES, LANES), LANES)] = (sh0[c] * conv[c]).astype(BF16)

        @pl.when(core == 0)
        def _():
            send_across(c, chan, 0)
            send_along(c, chan, 1)

        @pl.when(core == 1)
        def _():
            send_along(c, chan, 0)
            send_across(c, chan, 1)

    def gated_here(c, part, blocks):
        copied(gated.at[c, :, pl.ds(0, blocks * LANES)], gate_recv.at[c, part])

    def relay_gated(c):
        @pl.when(core == 0)
        def _():
            gated_here(c, 0, 1)
            send_along(c, (1 - xhi) * YS + y, 1)

        @pl.when(core == 1)
        def _():
            gated_here(c, 0, 3)
            for y_ in y_mates:
                send_across(c, xhi * YS + y_, 1)

    def add_out(c):
        @pl.when(core == 0)
        def _():
            gated_here(c, 1, 6)

        @pl.when(core == 1)
        def _():
            gated_here(c, 1, 4)

        part = jnp.dot(gated[c], wt[c], preferred_element_type=F32)
        if c == 0:
            acc[...] = part
        elif c < CHUNKS - 1:
            acc[...] += part
        else:
            out[...] = (acc[...] + part).astype(BF16)


    units = range(len(UNITS))
    for u, (streams, first, count) in enumerate(UNITS):
        for i, j in enumerate(streams):
            width = count * LANES
            pltpu.make_async_copy(
                w_in.at[j, :, first * LANES:first * LANES + width],
                rows(u, z, x, core, 0, BLOCK).at[:, i * width:(i + 1) * width],
                local_sem.at[0],
            ).start()
    own_tokens = pltpu.make_async_copy(tokens, tok.at[pl.ds(HALO, ROWS)], local_sem.at[1])
    own_tokens.start()
    own_columns = pltpu.make_async_copy(
        wt_columns(slice(None), chan), wt_slot(slice(None), chan), local_sem.at[2]
    )
    own_columns.start()
    parameters = [
        pltpu.make_async_copy(src, dst, local_sem.at[3 + i])
        for i, (src, dst) in enumerate(
            ((taps_hbm, taps), (residues_hbm, residues), (decays_hbm, decays), (skip_hbm, skip))
        )
    ]
    for copy in parameters:
        copy.start()

    barrier = pltpu.get_barrier_semaphore()
    planes = [at(lax.rem(z + d, PLANES), x, core, xhi, y) for d in (4, 3, 5, 2, 6, 1, 7)]
    greeted = planes + diagonals + [across] + [at(z, x, core, xhi, y_) for y_ in y_mates] + mates
    greeted += [next_slab, (lax.rem(slab + SLABS - 1, SLABS), chan)]
    for device in greeted:
        pl.semaphore_signal(barrier, inc=1, device_id=device, device_id_type=MESH)
    pl.semaphore_wait(barrier, len(greeted))

    def start_columns():
        start(tokens.at[pl.ds(ROWS - HALO, HALO)], tok.at[pl.ds(0, HALO)], halo_sem.at[0], halo_sem.at[1], next_slab)
        wt_start()

    copied(wbufs[0].at[pl.ds(0, BLOCK * 3 * WIDTH // wbufs[0].shape[1])], local_sem.at[0])

    def halo_here():
        own_tokens.wait()
        for copy in parameters:
            copy.wait()
        copied(tok.at[pl.ds(0, HALO)], halo_sem.at[1])

    def columns_here():
        own_columns.wait()
        wt_relay()
        copied(wt.at[mine, pl.ds(0, 7 * LANES)], wt_core)

    work = {}

    def plan(when, rank, part):
        work.setdefault(when, []).append((rank, len(work.get(when, [])), part))

    def unit_of(stream, c):
        return next(u for u in units if stream in UNITS[u][0] and UNITS[u][1] <= c < UNITS[u][1] + UNITS[u][2])

    plan(0, 0, start_columns)
    plan(OPENED[0] + 5, 0, halo_here)
    for u in units:
        plan(OPENED[u] + 5, 1 + u, functools.partial(project, u))
    last = 0
    for c in range(CHUNKS):
        when = OPENED[unit_of(1, c)] + 5 + PLANE_LAG
        plan(when, 0, functools.partial(plane_states, c))
        when += ENTER_LAG
        plan(when, 20, functools.partial(enter, c))
        u = unit_of(0, c)
        rank = 21
        if OPENED[u] + 5 > when:
            when, rank = OPENED[u] + 5, 1.5 + u
        plan(when, rank, functools.partial(gate, c))
        plan(when + RELAY_LAG, 30 + c, functools.partial(relay_gated, c))
        last = max(last + 1, when + OUT_LAG)
        plan(last, 40 + c, functools.partial(add_out, c))
        if c == 0:
            plan(last, 0, columns_here)

    for t in range(last + 1):
        opened = [u for u in units if OPENED[u] == t]
        if t == 0:
            for u in units:
                inject(u)
        for u in opened:
            if u > opened[0] and STAGGERED:
                own_sent(u - 1)
            own_first(u)
            if STAGGERED:
                own_second(u)
        for u in units:
            if 1 <= t - OPENED[u] <= 4:
                ring(u, t - OPENED[u])
        for u in opened:
            if not STAGGERED:
                own_second(u)
        for u in units:
            if t - OPENED[u] == 5:
                cross(u)
        for _, _, part in sorted(work.get(t, []), key=lambda entry: entry[:2]):
            part()

    copied(tok.at[pl.ds(0, HALO)], halo_sem.at[0])
    copied(wt.at[mine, pl.ds(0, 7 * LANES)], wt_send)
    copied(wt.at[mine, pl.ds(0, 7 * LANES)], wt_core_send)
    for u in units:
        if not (STAGGERED and u + 1 < len(UNITS) and OPENED[u + 1] == OPENED[u]):
            own_sent(u)
        copied(wbufs[u].at[pl.ds(0, 5 * BLOCK + 7 * HALF + 9 * HALF + DEPTH // 2)], w_send.at[u])
    for c in range(CHUNKS):
        copied(gated.at[c, :, pl.ds(0, 7 * LANES)], gate_send.at[c])
        copied(est.at[c, pl.ds(0, 3)], est_send.at[c])
        copied(pst.at[c, pl.ds(0, PLANES - 1)], pst_send.at[c])


def body(tokens, w_in, short_taps, residues, decay_rates, skip_gain, w_out):
    any_space = pl.BlockSpec(memory_space=pl.ANY)
    vmem = pl.BlockSpec(memory_space=pltpu.VMEM)
    dma = pltpu.SemaphoreType.DMA
    units = len(UNITS)
    return pl.pallas_call(
        kernel,
        out_shape=jax.ShapeDtypeStruct((ROWS, WIDTH), BF16),
        in_specs=[any_space] * 7,
        out_specs=vmem,
        scratch_shapes=[
            pltpu.VMEM((3, 3, WIDTH), F32),
            pltpu.VMEM((MODES, WIDTH), F32),
            pltpu.VMEM((MODES, WIDTH), F32),
            pltpu.VMEM((1, WIDTH), F32),
            [pltpu.VMEM((DEPTH, len(streams) * count * LANES), BF16) for streams, _, count in UNITS],
            pltpu.VMEM((HALO + ROWS, DEPTH), BF16),
            pltpu.VMEM((CHUNKS, CHANS * LANES, WIDTH), BF16),
            pltpu.VMEM((HALO + ROWS, WIDTH), F32),
            pltpu.VMEM((CHUNKS, ROWS, LANES), F32),
            pltpu.VMEM((CHUNKS, ROWS, LANES), F32),
            pltpu.VMEM((CHUNKS, ROWS, LANES), F32),
            pltpu.VMEM((CHUNKS, MODES, SEGS, LANES), F32),
            pltpu.VMEM((CHUNKS, 4, MODES, LANES), F32),
            pltpu.VMEM((CHUNKS, PLANES, MODES, LANES), F32),
            pltpu.VMEM((CHUNKS, ROWS, CHANS * LANES), BF16),
            pltpu.VMEM((ROWS, WIDTH), F32),
            dma((7,)),
            dma((units,)),
            dma((units, 4, 2)),
            dma((units, 3, 2)),
            dma((units,)),
            dma((units,)),
            dma((units,)),
            dma((units,)),
            dma((2,)),
            dma((CHUNKS,)),
            dma((CHUNKS,)),
            dma((CHUNKS,)),
            dma((CHUNKS,)),
            dma((CHUNKS,)),
            dma((CHUNKS, 2)),
            dma,
            dma,
            dma,
            dma,
        ],
        compiler_params=pltpu.CompilerParams(
            collective_id=0, has_side_effects=True, vmem_limit_bytes=56 << 20
        ),
        cost_estimate=pl.CostEstimate(flops=5 * 10**9, bytes_accessed=10**7, transcendentals=0),
        name="hyena",
    )(
        tokens,
        w_in.transpose(1, 0, 2),
        short_taps,
        residues,
        decay_rates,
        skip_gain.reshape(1, WIDTH),
        w_out,
    )


def solution(mesh):
    return jax.shard_map(
        body,
        mesh=mesh,
        in_specs=(
            P("seq", None),
            P("seq", None, "chan"),
            P(None, None, "chan"),
            P(None, "chan"),
            P(None, "chan"),
            P("chan"),
            P("chan", None),
        ),
        out_specs=P("seq", "chan"),
        check_vma=False,
    )
```

```python
import functools

import jax
import jax.numpy as jnp
from jax import lax
from jax.experimental import pallas as pl
from jax.experimental.pallas import tpu as pltpu
from jax.sharding import PartitionSpec as P

MESH = pl.DeviceIdType.MESH
F32, BF16 = jnp.float32, jnp.bfloat16

PLANES = 8
YS = 4
SLABS = 32
CHANS = 8
CHUNKS = 4
LANES = 128
WIDTH = CHUNKS * LANES
DEPTH = 4096
BLOCK = DEPTH // SLABS
HALF = BLOCK // 2
ROWS = 256
HALO = 16
SEGS = 8
SEG = ROWS // SEGS
MODES = 16
UNITS = (
    ((1, 2), 0, 1),
    ((1, 2), 1, 1),
    ((0,), 0, 1),
    ((1, 2), 2, 1),
    ((1, 2), 3, 1),
    ((0,), 1, 1),
    ((0,), 2, 1),
    ((0,), 3, 1),
)
OPENED = (0, 1, 2, 3, 4, 5, 6, 7)
STAGGERED = True
PLANE_LAG, ENTER_LAG, RELAY_LAG, OUT_LAG = 1, 2, 1, 2


def copied(ref, sem):
    pltpu.make_async_copy(ref, ref, sem).wait()


def kernel(
    tokens, w_in, taps_hbm, residues_hbm, decays_hbm, skip_hbm, w_out, out,
    taps, residues, decays, skip, wbufs, tok, wt, pj, sh0, prod, conv, hseg, est, pst, gated, acc,
    local_sem, w_send, w_major, w_minor, w_cross, w_inject, w_core, w_own,
    halo_sem, est_send, est_recv, pst_send, pst_recv, gate_send, gate_recv,
    wt_send, wt_recv, wt_core, wt_core_send,
):
    slab, chan = lax.axis_index("seq"), lax.axis_index("chan")
    z, spot = slab // 4, lax.rem(slab, 4)
    x, core = spot // 2, lax.rem(spot, 2)
    xhi, y = chan // YS, lax.rem(chan, YS)
    sign = 1 - 2 * core

    def at(z_, x_, core_, xhi_, y_):
        return (z_ * 4 + x_ * 2 + core_, xhi_ * YS + y_)

    def turned(distance):
        return lax.rem(z + distance * sign + 2 * PLANES, PLANES)

    ahead, behind = at(turned(1), x, core, xhi, y), at(turned(-1), x, core, xhi, y)
    beside, twin = at(z, 1 - x, core, xhi, y), at(z, x, 1 - core, xhi, y)
    across = at(z, x, core, 1 - xhi, y)
    mates = [at(z, x, 1 - core, xhi, y), at(z, 1 - x, core, xhi, y), at(z, 1 - x, 1 - core, xhi, y)]
    next_slab = (lax.rem(slab + 1, SLABS), chan)
    y_mates = [lax.rem(y + d, YS) for d in (1, 3, 2)]
    diagonals = [at(z, 1 - x, core, 1 - xhi, y_) for y_ in range(YS)]

    def start(src, dst, send, recv, device):
        pltpu.make_async_remote_copy(
            src_ref=src, dst_ref=dst, send_sem=send, recv_sem=recv, device_id=device, device_id_type=MESH
        ).start()


    def rows(c, z_, x_, core_, first, count):
        begin = pl.multiple_of((z_ * 4 + x_ * 2 + core_) * BLOCK + first, HALF)
        return wbufs[c].at[pl.ds(begin, count)]

    def w_copy(c, ref, device, recv):
        start(ref, ref, w_send.at[c], recv, device)

    def main_rows(c, z_):
        return rows(c, z_, x, core, 0, BLOCK)

    def carried_rows(c, z_):
        return rows(c, z_, 1 - x, core, 0, HALF)

    def to_core(c, ref):
        w_copy(c, ref, twin, w_core.at[c])

    def inject(c):
        w_copy(c, rows(c, z, x, core, 0, HALF), beside, w_inject.at[c])

    def own_first(c):
        block = main_rows(c, z)
        start(block, block, w_own.at[c], w_major.at[c, 0, 0], ahead)
        start(block, block, w_own.at[c], w_minor.at[c, 0, 0], behind)
        w_copy(c, rows(c, z, x, core, HALF, HALF), beside, w_cross.at[c])
        to_core(c, main_rows(c, z))

    def own_sent(c):
        copied(wbufs[c].at[pl.ds(0, 2 * BLOCK)], w_own.at[c])

    def own_second(c):
        block = carried_rows(c, z)
        copied(block, w_inject.at[c])
        w_copy(c, block, ahead, w_major.at[c, 0, 1])
        w_copy(c, block, behind, w_minor.at[c, 0, 1])
        to_core(c, block)

    def ring(c, j):
        for part, of in ((0, main_rows), (1, carried_rows)):
            for sems, device, last, source in (
                (w_major, ahead, 4, turned(-j)),
                (w_minor, behind, 3, turned(j)),
            ):
                if j > last:
                    continue
                block = of(c, source)
                copied(block, sems.at[c, j - 1, part])
                if j < last:
                    w_copy(c, block, device, sems.at[c, j, part])
                if part == 0:
                    w_copy(c, rows(c, source, x, core, HALF, HALF), beside, w_cross.at[c])
                to_core(c, block)

    def cross(c):
        copied(wbufs[c].at[pl.ds(0, PLANES * HALF)], w_cross.at[c])
        for source in range(PLANES):
            to_core(c, rows(c, source, 1 - x, core, HALF, HALF))


    w_out_chunks = w_out.reshape(CHUNKS, LANES, DEPTH)
    mine = pl.ds(core * 2, 2)

    def wt_slot(part, source):
        return wt.at[part, pl.ds(pl.multiple_of(source * LANES, LANES), LANES)]

    def wt_columns(part, target):
        return w_out_chunks.at[part, :, pl.ds(pl.multiple_of(target * 512, 512), 512)]

    wt_peers = [(xhi * YS + y_, at(z, x, core, xhi, y_)) for y_ in y_mates]
    wt_peers += [((1 - xhi) * YS + y_, diagonals[y_]) for y_ in range(YS)]

    def wt_start():
        for target, device in wt_peers:
            start(wt_columns(mine, target), wt_slot(mine, chan), wt_send, wt_recv, device)

    def wt_relay():
        copied(wt.at[mine, pl.ds(0, 7 * LANES)], wt_recv)
        for source, _ in wt_peers:
            start(wt_slot(mine, source), wt_slot(mine, source), wt_core_send, wt_core, twin)


    def lanes(ref, row, c):
        return ref[pl.ds(row, 1), c * LANES:(c + 1) * LANES]

    def project(u):
        copied(wbufs[u].at[pl.ds(0, DEPTH // 2)], w_core.at[u])
        width = wbufs[u].shape[1]
        result = jnp.dot(tok[...], wbufs[u][...], preferred_element_type=F32)
        pj[:, :width] = result.astype(BF16).astype(F32)

        @pl.when(slab == 0)
        def _():
            pj[pl.ds(0, HALO), :width] = jnp.zeros((HALO, width), F32)

        streams, first, count = UNITS[u]

        def shorted(j, c):
            column = streams.index(j) * count + c - first
            total = None
            for a in range(3):
                tap = taps[a, pl.ds(j, 1), c * LANES:(c + 1) * LANES]
                term = tap * pj[pl.ds(HALO - a, ROWS), column * LANES:(column + 1) * LANES]
                total = term if total is None else total + term
            return total

        for c in range(first, first + count):
            if 0 in streams:
                sh0[c] = shorted(0, c)
            if 1 in streams:
                prod[c] = shorted(1, c) * shorted(2, c)
                recur(c)
                send_states(c)

    def mode_lanes(c, m):
        rate = jnp.broadcast_to(lanes(decays, m, c), (SEGS, LANES))
        size = jnp.broadcast_to(lanes(residues, m, c), (SEGS, LANES))
        return rate, size

    def added(parts):
        parts = list(parts)
        while len(parts) > 1:
            parts = [a + b for a, b in zip(parts[::2], parts[1::2])]
        return parts[0]

    def recur(c):
        factors, gains = [], []
        for m in range(MODES):
            rate, size = mode_lanes(c, m)
            factors.append(jnp.exp(-rate))
            gains.append(size * jnp.sqrt(rate * (2.0 / MODES)))

        def step(i, states):
            place = pl.ds(i, SEGS, stride=SEG)
            value = prod[c, place, :]
            states = tuple(f * s + g * value for f, g, s in zip(factors, gains, states))
            conv[c, place, :] = added(states)
            return states

        states = lax.fori_loop(0, SEG, step, (jnp.zeros((SEGS, LANES), F32),) * MODES, unroll=4)
        segment = lax.broadcasted_iota(jnp.int32, (SEGS, LANES), 0)
        for m in range(MODES):
            rate, _ = mode_lanes(c, m)
            total = states[m]
            for shift in (1, 2, 4):
                earlier = jnp.where(segment >= shift, pltpu.roll(total, shift, 0), 0.0)
                total = total + jnp.exp(rate * (-float(SEG * shift))) * earlier
            hseg[c, m] = jnp.where(segment >= 1, pltpu.roll(total, 1, 0), 0.0)
            est[c, spot, pl.ds(m, 1)] = total[SEGS - 1:]

    def send_states(c):
        block = est.at[c, spot]
        for device in mates:
            start(block, block, est_send.at[c], est_recv.at[c], device)

    def slab_factor(c, slabs):
        return jnp.exp(decays[:, c * LANES:(c + 1) * LANES] * (-float(ROWS * slabs)))

    def plane_states(c):
        copied(est.at[c, pl.ds(0, 3)], est_recv.at[c])
        factor = slab_factor(c, 1)
        total = est[c, 0]
        for q in range(1, 4):
            total = factor * total + est[c, q]
        pst[c, z] = total
        block = pst.at[c, z]

        for d in (4, 3, 5, 2, 6, 1, 7):
            device = at(lax.rem(z + d, PLANES), x, core, xhi, y)
            start(block, block, pst_send.at[c], pst_recv.at[c], device)

    def enter(c):
        factor, plane_factor = slab_factor(c, 1), slab_factor(c, 4)

        copied(pst.at[c, pl.ds(0, PLANES - 1)], pst_recv.at[c])
        total = jnp.zeros((MODES, LANES), F32)
        for earlier in range(PLANES - 1):
            total = jnp.where(earlier < z, plane_factor * total + pst[c, earlier], total)
        for q in range(3):
            total = jnp.where(q < spot, factor * total + est[c, q], total)
        segment = lax.broadcasted_iota(jnp.int32, (SEGS, LANES), 0).astype(F32)
        factors, states = [], []
        for m in range(MODES):
            rate, _ = mode_lanes(c, m)
            factors.append(jnp.exp(-rate))
            entering = jnp.broadcast_to(total[m:m + 1], (SEGS, LANES))
            states.append(hseg[c, m] + jnp.exp(rate * (segment * -float(SEG))) * entering)

        def step(i, states):
            states = tuple(f * s for f, s in zip(factors, states))
            place = pl.ds(i, SEGS, stride=SEG)
            conv[c, place, :] = conv[c, place, :] + added(states)
            return states

        lax.fori_loop(0, SEG, step, tuple(states), unroll=4)
        conv[c] = conv[c] + lanes(skip, 0, c) * prod[c]

    def gate_slot(c, source):
        return gated.at[c, :, pl.ds(pl.multiple_of(source * LANES, LANES), LANES)]


    def send_across(c, source, part):
        block = gate_slot(c, source)
        start(block, block, gate_send.at[c], gate_recv.at[c, part], across)

    def send_along(c, source, part):
        block = gate_slot(c, source)
        for y_ in y_mates:
            start(block, block, gate_send.at[c], gate_recv.at[c, part], at(z, x, core, xhi, y_))

    def gate(c):
        gated[c, :, pl.ds(pl.multiple_of(chan * LANES, LANES), LANES)] = (sh0[c] * conv[c]).astype(BF16)

        @pl.when(core == 0)
        def _():
            send_across(c, chan, 0)
            send_along(c, chan, 1)

        @pl.when(core == 1)
        def _():
            send_along(c, chan, 0)
            send_across(c, chan, 1)

    def gated_here(c, part, blocks):
        copied(gated.at[c, :, pl.ds(0, blocks * LANES)], gate_recv.at[c, part])

    def relay_gated(c):
        @pl.when(core == 0)
        def _():
            gated_here(c, 0, 1)
            send_along(c, (1 - xhi) * YS + y, 1)

        @pl.when(core == 1)
        def _():
            gated_here(c, 0, 3)
            for y_ in y_mates:
                send_across(c, xhi * YS + y_, 1)

    def add_out(c):
        @pl.when(core == 0)
        def _():
            gated_here(c, 1, 6)

        @pl.when(core == 1)
        def _():
            gated_here(c, 1, 4)

        part = jnp.dot(gated[c], wt[c], preferred_element_type=F32)
        if c == 0:
            acc[...] = part
        elif c < CHUNKS - 1:
            acc[...] += part
        else:
            out[...] = (acc[...] + part).astype(BF16)


    units = range(len(UNITS))
    for u, (streams, first, count) in enumerate(UNITS):
        for i, j in enumerate(streams):
            width = count * LANES
            pltpu.make_async_copy(
                w_in.at[j, :, first * LANES:first * LANES + width],
                rows(u, z, x, core, 0, BLOCK).at[:, i * width:(i + 1) * width],
                local_sem.at[0],
            ).start()
    own_tokens = pltpu.make_async_copy(tokens, tok.at[pl.ds(HALO, ROWS)], local_sem.at[1])
    own_tokens.start()
    own_columns = pltpu.make_async_copy(
        wt_columns(slice(None), chan), wt_slot(slice(None), chan), local_sem.at[2]
    )
    own_columns.start()
    parameters = [
        pltpu.make_async_copy(src, dst, local_sem.at[3 + i])
        for i, (src, dst) in enumerate(
            ((taps_hbm, taps), (residues_hbm, residues), (decays_hbm, decays), (skip_hbm, skip))
        )
    ]
    for copy in parameters:
        copy.start()

    barrier = pltpu.get_barrier_semaphore()
    planes = [at(lax.rem(z + d, PLANES), x, core, xhi, y) for d in (4, 3, 5, 2, 6, 1, 7)]
    greeted = planes + diagonals + [across] + [at(z, x, core, xhi, y_) for y_ in y_mates] + mates
    greeted += [next_slab, (lax.rem(slab + SLABS - 1, SLABS), chan)]
    for device in greeted:
        pl.semaphore_signal(barrier, inc=1, device_id=device, device_id_type=MESH)
    pl.semaphore_wait(barrier, len(greeted))

    def start_columns():
        start(tokens.at[pl.ds(ROWS - HALO, HALO)], tok.at[pl.ds(0, HALO)], halo_sem.at[0], halo_sem.at[1], next_slab)
        wt_start()

    copied(wbufs[0].at[pl.ds(0, BLOCK * 3 * WIDTH // wbufs[0].shape[1])], local_sem.at[0])

    def halo_here():
        own_tokens.wait()
        for copy in parameters:
            copy.wait()
        copied(tok.at[pl.ds(0, HALO)], halo_sem.at[1])

    def columns_here():
        own_columns.wait()
        copied(wt.at[mine, pl.ds(0, 7 * LANES)], wt_core)

    work = {}

    def plan(when, rank, part):
        work.setdefault(when, []).append((rank, len(work.get(when, [])), part))

    def unit_of(stream, c):
        return next(u for u in units if stream in UNITS[u][0] and UNITS[u][1] <= c < UNITS[u][1] + UNITS[u][2])

    plan(0, 0, start_columns)
    plan(OPENED[0] + 5, 0, halo_here)
    for u in units:
        plan(OPENED[u] + 5, 1 + u, functools.partial(project, u))
    last = 0
    for c in range(CHUNKS):
        when = OPENED[unit_of(1, c)] + 5 + PLANE_LAG
        plan(when, 0, functools.partial(plane_states, c))
        when += ENTER_LAG
        plan(when, 20, functools.partial(enter, c))
        u = unit_of(0, c)
        rank = 21
        if OPENED[u] + 5 > when:
            when, rank = OPENED[u] + 5, 1.5 + u
        plan(when, rank, functools.partial(gate, c))
        plan(when + RELAY_LAG, 30 + c, functools.partial(relay_gated, c))
        last = max(last, when + OUT_LAG)
    plan(OPENED[0] + 8, 25, wt_relay)
    plan(last, 39, columns_here)
    for c in range(CHUNKS):
        plan(last, 40 + c, functools.partial(add_out, c))

    for t in range(last + 1):
        opened = [u for u in units if OPENED[u] == t]
        if t == 0:
            for u in units:
                inject(u)
        for u in opened:
            if u > opened[0] and STAGGERED:
                own_sent(u - 1)
            own_first(u)
            if STAGGERED:
                own_second(u)
        for u in units:
            if 1 <= t - OPENED[u] <= 4:
                ring(u, t - OPENED[u])
        for u in opened:
            if not STAGGERED:
                own_second(u)
        for u in units:
            if t - OPENED[u] == 5:
                cross(u)
        for _, _, part in sorted(work.get(t, []), key=lambda entry: entry[:2]):
            part()

    copied(tok.at[pl.ds(0, HALO)], halo_sem.at[0])
    copied(wt.at[mine, pl.ds(0, 7 * LANES)], wt_send)
    copied(wt.at[mine, pl.ds(0, 7 * LANES)], wt_core_send)
    for u in units:
        if not (STAGGERED and u + 1 < len(UNITS) and OPENED[u + 1] == OPENED[u]):
            own_sent(u)
        copied(wbufs[u].at[pl.ds(0, 5 * BLOCK + 7 * HALF + 9 * HALF + DEPTH // 2)], w_send.at[u])
    for c in range(CHUNKS):
        copied(gated.at[c, :, pl.ds(0, 7 * LANES)], gate_send.at[c])
        copied(est.at[c, pl.ds(0, 3)], est_send.at[c])
        copied(pst.at[c, pl.ds(0, PLANES - 1)], pst_send.at[c])


def body(tokens, w_in, short_taps, residues, decay_rates, skip_gain, w_out):
    any_space = pl.BlockSpec(memory_space=pl.ANY)
    vmem = pl.BlockSpec(memory_space=pltpu.VMEM)
    dma = pltpu.SemaphoreType.DMA
    units = len(UNITS)
    return pl.pallas_call(
        kernel,
        out_shape=jax.ShapeDtypeStruct((ROWS, WIDTH), BF16),
        in_specs=[any_space] * 7,
        out_specs=vmem,
        scratch_shapes=[
            pltpu.VMEM((3, 3, WIDTH), F32),
            pltpu.VMEM((MODES, WIDTH), F32),
            pltpu.VMEM((MODES, WIDTH), F32),
            pltpu.VMEM((1, WIDTH), F32),
            [pltpu.VMEM((DEPTH, len(streams) * count * LANES), BF16) for streams, _, count in UNITS],
            pltpu.VMEM((HALO + ROWS, DEPTH), BF16),
            pltpu.VMEM((CHUNKS, CHANS * LANES, WIDTH), BF16),
            pltpu.VMEM((HALO + ROWS, WIDTH), F32),
            pltpu.VMEM((CHUNKS, ROWS, LANES), F32),
            pltpu.VMEM((CHUNKS, ROWS, LANES), F32),
            pltpu.VMEM((CHUNKS, ROWS, LANES), F32),
            pltpu.VMEM((CHUNKS, MODES, SEGS, LANES), F32),
            pltpu.VMEM((CHUNKS, 4, MODES, LANES), F32),
            pltpu.VMEM((CHUNKS, PLANES, MODES, LANES), F32),
            pltpu.VMEM((CHUNKS, ROWS, CHANS * LANES), BF16),
            pltpu.VMEM((ROWS, WIDTH), F32),
            dma((7,)),
            dma((units,)),
            dma((units, 4, 2)),
            dma((units, 3, 2)),
            dma((units,)),
            dma((units,)),
            dma((units,)),
            dma((units,)),
            dma((2,)),
            dma((CHUNKS,)),
            dma((CHUNKS,)),
            dma((CHUNKS,)),
            dma((CHUNKS,)),
            dma((CHUNKS,)),
            dma((CHUNKS, 2)),
            dma,
            dma,
            dma,
            dma,
        ],
        compiler_params=pltpu.CompilerParams(
            collective_id=0, has_side_effects=True, vmem_limit_bytes=56 << 20
        ),
        cost_estimate=pl.CostEstimate(flops=5 * 10**9, bytes_accessed=10**7, transcendentals=0),
        name="hyena",
    )(
        tokens,
        w_in.transpose(1, 0, 2),
        short_taps,
        residues,
        decay_rates,
        skip_gain.reshape(1, WIDTH),
        w_out,
    )


def solution(mesh):
    return jax.shard_map(
        body,
        mesh=mesh,
        in_specs=(
            P("seq", None),
            P("seq", None, "chan"),
            P(None, None, "chan"),
            P(None, "chan"),
            P(None, "chan"),
            P("chan"),
            P("chan", None),
        ),
        out_specs=P("seq", "chan"),
        check_vma=False,
    )
```
